512 devices in a mesh: tm: 16 (over x, z_lo), tp: 32 (over z_hi, y, core).
Axes of the slice: x: 4, y: 8, z: 8 (z_hi: 2, z_lo: 4; z = z_hi * 4 + z_lo), core: 2. Of those that a mesh axis runs over, the one named last changes fastest.
Arguments:
- pixels: bfloat16 [32, 32, 32, 1176], P('tm', 'tp'), may hold values from -6 to 6
- conv_weight: bfloat16 [1176, 1280], P(None, 'tm'), may hold values from -0.1875 to 0.1875
- norm_gain: float32 [1280], replicated, may hold values from 0.1 to 1.9
- norm_bias: float32 [1280], replicated, may hold values from -3 to 3
- proj_in: bfloat16 [5120, 5120], P(None, 'tp'), may hold values from -0.078125 to 0.078125
- bias_in: float32 [5120], P('tp'), may hold values from -3 to 3
- proj_out: bfloat16 [5120, 8192], P(None, 'tp'), may hold values from -0.078125 to 0.078125
- bias_out: float32 [8192], P('tp'), may hold values from -3 to 3
Outputs:
- tokens_out: bfloat16 [32, 16, 16, 8192], P('tm', None, None, 'tp')
The draws below stay inside these ranges and needn't reach their ends.
All inputs are finite; a program needn't handle non-finite values.
Results may differ from the reference program's by a relative error of at most 0.0052.
Values may be sent and summed in bfloat16 or wider, within the bound.
No kernel may reach another device: no remote copies, remote signals or barrier semaphores. Data moves between devices by JAX's collectives and lax.ppermute only.
A program may use at most 64 MiB of HBM per device.

```python
import jax
import jax.numpy as jnp
from jax import lax

KP = 1176
C = 1280
HID = 5120
OUT = 8192
GH = 32
GW = 32
PAIRS = 32


def block_levels(key, shape, shards, low, top_value):
    loudness = 1.0
    for dim, shards_of in shards:
        draws = jax.random.uniform(jax.random.fold_in(jax.random.fold_in(key, 6), dim), (shards_of,), jnp.float32, low / len(shards), top_value / len(shards))
        loudness = loudness * jnp.repeat(jnp.exp(draws), shape[dim] // shards_of).reshape((-1,) + (1,) * (len(shape) - 1 - dim))
    return loudness


def normal_values(rng, shape, spread, bound, split=(), kind=jnp.bfloat16):
    entries = jax.random.normal(rng, shape, jnp.float32) * spread
    if len(split) > 0:
        entries = block_levels(rng, shape, split, -0.22, 0.18) * entries
    return jnp.clip(entries, min=-bound, max=bound).astype(kind)


def setup_inputs(seed: int = 0) -> dict:
    keys = jax.random.split(jax.random.key(seed), 9)
    pixels = normal_values(keys[0], (PAIRS, GH, GW, KP), 1.0, 6.0, ((0, 16), (1, 32)))
    conv_weight = normal_values(keys[1], (KP, C), KP ** -0.5, 0.1875, ((1, 16),))
    norm_gain = jnp.clip(1.0 + 0.18 * jax.random.normal(keys[2], (C,), jnp.float32), 0.1, 1.9)
    norm_bias = normal_values(keys[3], (C,), 0.3, 3.0, (), jnp.float32)
    proj_in = normal_values(keys[4], (HID, HID), HID ** -0.5, 0.078125, ((1, 32),))
    bias_in = normal_values(keys[5], (HID,), 0.5, 3.0, ((0, 32),), jnp.float32)
    proj_out = normal_values(keys[6], (HID, OUT), HID ** -0.5, 0.078125, ((1, 32),))
    bias_out = normal_values(keys[7], (OUT,), 0.5, 3.0, ((0, 32),), jnp.float32)
    return dict(pixels=pixels, conv_weight=conv_weight, norm_gain=norm_gain, norm_bias=norm_bias, proj_in=proj_in, bias_in=bias_in, proj_out=proj_out, bias_out=bias_out)


def one_pair(frame, conv_weight, norm_gain, norm_bias, proj_in, bias_in, proj_out, bias_out):
    flat = frame.reshape(GH * GW, KP)
    embed = jnp.dot(flat, conv_weight, preferred_element_type=jnp.float32)
    mean = lax.optimization_barrier(jnp.mean(embed, axis=-1, keepdims=True))
    centred = embed - mean
    variance = lax.optimization_barrier(jnp.mean(centred * centred, axis=-1, keepdims=True))
    normed = (centred * lax.rsqrt(variance + 1e-06) * norm_gain + norm_bias).astype(jnp.bfloat16)
    blocks = normed.reshape(GH // 2, 2, GW // 2, 2, C).transpose(0, 2, 1, 3, 4)
    merged = blocks.reshape(GH // 2 * (GW // 2), HID)
    hidden = jax.nn.gelu(jnp.dot(merged, proj_in, preferred_element_type=jnp.float32) + bias_in, approximate=False).astype(jnp.bfloat16)
    result = jnp.dot(hidden, proj_out, preferred_element_type=jnp.float32) + bias_out
    return result.astype(jnp.bfloat16).reshape(GH // 2, GW // 2, OUT)

def reference(pixels, conv_weight, norm_gain, norm_bias, proj_in, bias_in, proj_out, bias_out):

    def step(frame):
        return one_pair(frame, conv_weight, norm_gain, norm_bias, proj_in, bias_in, proj_out, bias_out)
    return lax.map(step, pixels)
```

```python
import functools

import jax
import jax.numpy as jnp
from jax import lax
from jax.experimental import pallas as pl
from jax.experimental.pallas import tpu as pltpu
from jax.sharding import Mesh, PartitionSpec as P

BF = jnp.bfloat16
F32 = jnp.float32
KP, C, HID = 1176, 1280, 5120
NX, NZ, NY = 4, 4, 8
PART = 320
TOK = 256


def shift(v, axis, n, by):
    return lax.ppermute(v, axis, [(i, (i + by) % n) for i in range(n)])


def shift_cores(v, axis, by):
    if axis == "x":
        pairs = [
            (2 * x + c, 2 * ((x + (by if c else -by)) % NX) + c) for x in range(NX) for c in range(2)
        ]
        return lax.ppermute(v, ("x", "c"), pairs)

    def at(z, c):
        z = z % 8
        return ((z % 4) * 2 + z // 4) * 2 + c

    pairs = [(at(z, c), at(z + (by if c else -by), c)) for z in range(8) for c in range(2)]
    return lax.ppermute(v, ("zl", "zh", "c"), pairs)


def embed_kernel(where, px, wt, *refs):
    sets = refs[:8]
    gain, beta, p_own, p_oth, b_in, out, xs, ws, ps, acc, sems = refs[8:]
    x, zl, core = where[0], where[2], where[3]
    copies = []

    def load(src, dst):
        c = pltpu.make_async_copy(src, dst, sems.at[len(copies)])
        c.start()
        copies.append(c)

    load(px, xs)
    for n in range(8):
        ahead = (0, 3, 1, 2)[n // 2]
        holder = core if n % 2 == 0 else 1 - core
        base = lax.rem(x + ahead, NX) * PART
        near = base + lax.rem(zl + 1 + 2 * holder, NZ) * 80
        load(sets[n].at[pl.ds(0, 80)], ws.at[pl.ds(pl.multiple_of(near, 16), 80)])
        for k in range(2):
            blk = base + lax.rem(zl + 2 * (1 - k), NZ) * 80
            src = pl.multiple_of(80 + 48 * k + 16 * holder, 16)
            dst = pl.multiple_of(blk + 48 * holder, 16)
            load(sets[n].at[pl.ds(src, 32)], ws.at[pl.ds(dst, 32)])
            if n % 2 == 0:
                src = pl.multiple_of(80 + 48 * k + 32 * (1 - core), 16)
                dst = pl.multiple_of(blk + 32, 16)
                load(sets[n].at[pl.ds(src, 16)], ws.at[pl.ds(dst, 16)])
    first_use = len(copies)
    load(p_own, ps.at[pl.ds(pl.multiple_of(core * 160, 32), 160)])
    load(p_oth, ps.at[pl.ds(pl.multiple_of((1 - core) * 160, 32), 160)])
    for c in copies[:first_use]:
        c.wait()
    g = gain[...]
    b = beta[...]
    for ij in range(4):
        patches = xs[:, ij].reshape(TOK, KP)
        e = lax.dot_general(patches, ws[...], (((1,), (1,)), ((), ())), preferred_element_type=F32)
        mean = jnp.sum(e, axis=-1, keepdims=True) * (1.0 / C)
        cen = e - mean
        var = jnp.sum(cen * cen, axis=-1, keepdims=True) * (1.0 / C)
        normed = (cen * lax.rsqrt(var + 1e-06) * g + b).astype(BF)
        if ij == 0:
            for c in copies[first_use:]:
                c.wait()
        part = lax.dot_general(
            normed,
            ps[:, ij * C : (ij + 1) * C],
            (((1,), (1,)), ((), ())),
            preferred_element_type=F32,
        )
        if ij == 0:
            acc[...] = part
        else:
            acc[...] += part
    pre = acc[...] + b_in[...]
    h = 0.5 * pre * (1.0 + lax.erf(pre * (0.5**0.5)))
    hs = [h[n * 16 : n * 16 + 16] for n in range(16)]
    top = jnp.concatenate(hs[0::2], axis=0)
    low = jnp.concatenate(hs[1::2], axis=0)
    out[:, :256] = top[:, :256].astype(BF)
    out[:, 256:320] = top[:, 256:].astype(BF)
    out[:, 320:384] = low[:, 256:].astype(BF)
    out[:, 384:] = low[:, :256].astype(BF)


def embed_hidden(where, px, wt, sets, gain, beta, p_own, p_oth, b_in):
    any_ = pl.BlockSpec(memory_space=pl.ANY)
    vmem = pl.BlockSpec(memory_space=pltpu.VMEM)
    return pl.pallas_call(
        embed_kernel,
        out_shape=jax.ShapeDtypeStruct((TOK // 2, 2 * PART), BF),
        in_specs=[pl.BlockSpec(memory_space=pltpu.SMEM)]
        + [any_] * 10
        + [vmem, vmem, any_, any_, vmem],
        out_specs=vmem,
        scratch_shapes=[
            pltpu.VMEM((16, 4, 16, KP), BF),
            pltpu.VMEM((C, KP), BF),
            pltpu.VMEM((PART, HID), BF),
            pltpu.VMEM((TOK, PART), F32),
            pltpu.SemaphoreType.DMA((40,)),
        ],
        compiler_params=pltpu.CompilerParams(vmem_limit_bytes=48 << 20),
        cost_estimate=pl.CostEstimate(
            flops=2 * (1024 * KP * C + TOK * HID * PART), bytes_accessed=12 << 20, transcendentals=0
        ),
        name="embed_hidden",
    )(where, px, wt, *sets, gain, beta, p_own, p_oth, b_in)


def out_kernel(where, near, *refs):
    hs = refs[:NY]
    p_own, p_oth, b_own, b_oth, o_own, o_oth, hv, pv0, pv1, acc, sems = refs[NY:]
    y, zh = where[1], where[4]
    loads = []
    for n, d in enumerate((0, -1, -2, -3, -4, 1, 2, 3) + tuple(range(NY))):
        if n < NY:
            shard = (1 - zh) * NY + lax.rem(y + (d + NY), NY)
            src = hs[n]
        else:
            shard = zh * NY + d
            src = near.at[d]
        rows = pl.ds(pl.multiple_of(shard * PART, 64), PART)
        loads.append(
            [
                pltpu.make_async_copy(p_own.at[rows], pv0.at[n], sems.at[3 * n]),
                pltpu.make_async_copy(p_oth.at[rows], pv1.at[n], sems.at[3 * n + 1]),
                pltpu.make_async_copy(src, hv.at[n], sems.at[3 * n + 2]),
            ]
        )
        for c in loads[n]:
            c.start()
    lane = lax.broadcasted_iota(jnp.int32, (TOK // 2, 128), 1)
    for n in range(2 * NY):
        for c in loads[n]:
            c.wait()
        h = hv[n]
        both = jnp.concatenate([h[:, :256], h[:, 384:]], axis=0)
        mid = h[:, 256:384]
        top = jnp.where(lane < 64, mid.astype(F32), 0.0).astype(BF)[:, :64]
        low = jnp.where(lane >= 64, mid.astype(F32), 0.0).astype(BF)
        for k, pv in enumerate((pv0, pv1)):
            part = jnp.dot(both, pv[n, :256, :], preferred_element_type=F32)
            rest = [
                jnp.dot(top, pv[n, 256:, :], preferred_element_type=F32),
                jnp.dot(low, pv[n, 192:, :], preferred_element_type=F32),
            ]
            part = part + jnp.concatenate(rest, axis=0)
            if n == 0:
                acc[k] = part
            else:
                acc[k] += part
    o_own[...] = (acc[0] + b_own[...]).astype(BF)
    o_oth[...] = (acc[1] + b_oth[...]).astype(BF)


def project_out(where, near, hs, p_own, p_oth, b_own, b_oth):
    any_ = pl.BlockSpec(memory_space=pl.ANY)
    vmem = pl.BlockSpec(memory_space=pltpu.VMEM)
    return pl.pallas_call(
        out_kernel,
        out_shape=[jax.ShapeDtypeStruct((TOK, 256), BF)] * 2,
        in_specs=[pl.BlockSpec(memory_space=pltpu.SMEM)] + [any_] * 11 + [vmem] * 2,
        out_specs=[vmem] * 2,
        scratch_shapes=[
            pltpu.VMEM((2 * NY, TOK // 2, 2 * PART), BF),
            pltpu.VMEM((2 * NY, PART, 256), BF),
            pltpu.VMEM((2 * NY, PART, 256), BF),
            pltpu.VMEM((2, TOK, 256), F32),
            pltpu.SemaphoreType.DMA((6 * NY,)),
        ],
        compiler_params=pltpu.CompilerParams(vmem_limit_bytes=40 << 20),
        cost_estimate=pl.CostEstimate(
            flops=2 * TOK * HID * 512, bytes_accessed=9 << 20, transcendentals=0
        ),
        name="project_out",
    )(where, near, *hs, p_own, p_oth, b_own, b_oth)


def per_device(pixels, conv_weight, norm_gain, norm_bias, proj_in, bias_in, proj_out, bias_out):
    core = lax.axis_index("c")
    first = core == 0
    where = jnp.stack([lax.axis_index(a) for a in ("x", "y", "zl", "c", "zh")]).astype(jnp.int32)

    rows = pixels.reshape(2, 32, KP)
    keep = jnp.where(first, rows[0], rows[1])
    give = jnp.where(first, rows[1], rows[0])
    got = shift(give, "c", 2, 1)
    mine = jnp.stack([jnp.where(first, keep, got), jnp.where(first, got, keep)])
    mine = mine.reshape(2, 16, 2, KP).transpose(0, 2, 1, 3).reshape(4, 16, KP)
    half = lax.all_gather(mine, "zh", axis=0)
    px = lax.all_gather(half, "y", axis=0).reshape(16, 4, 16, KP)

    wt = conv_weight.T
    wt, _ = lax.optimization_barrier((wt, half))
    part = jnp.where(first, wt[:48], wt[32:])
    near = shift_cores(wt, "z", 1)
    two = shift_cores(part, "z", 2)
    held = jnp.concatenate([near, two, part], axis=0)
    prev = shift(held, "x", NX, 1)
    nxt = shift(held, "x", NX, -1)
    far = shift_cores(jnp.where(first, nxt, prev), "x", 1)
    sets = []
    for s in (held, prev, nxt, far):
        sets += [s, shift(s, "c", 2, 1)]

    p_in = proj_in.T
    p_in_o = shift(p_in, "c", 2, 1)
    p_out_o = shift(proj_out, "c", 2, 1)
    bias = jnp.concatenate([bias_in, bias_out]).reshape(1, -1)
    bias_o = shift(bias, "c", 2, 1)
    b0, b1 = bias[:, :160], bias_o[:, :160]
    b_in = jnp.concatenate([jnp.where(first, b0, b1), jnp.where(first, b1, b0)], axis=1)
    hid = embed_hidden(
        where,
        px,
        wt,
        sets,
        norm_gain.reshape(1, C),
        norm_bias.reshape(1, C),
        p_in,
        p_in_o,
        b_in,
    )
    g_near = lax.all_gather(hid, "y", axis=0)
    partner = shift(hid, "zh", 2, 1)
    right, left = [partner], [partner]
    for step in range(4):
        right.append(shift(right[-1], "y", NY, 1))
        if step < 3:
            left.append(shift(left[-1], "y", NY, -1))
    o_own, o_oth = project_out(
        where, g_near, right + left[1:], proj_out, p_out_o, bias[:, 160:], bias_o[:, 160:]
    )
    o_got = shift(o_oth, "c", 2, 1)
    result = jnp.stack([jnp.where(first, o_own, o_got), jnp.where(first, o_got, o_own)])
    return result.reshape(2, 16, 16, 256)


def solution(mesh):
    fine = Mesh(mesh.devices.reshape(NX, NZ, 2, NY, 2), ("x", "zl", "zh", "y", "c"))
    tm, tp = ("x", "zl"), ("zh", "y", "c")
    return jax.shard_map(
        per_device,
        mesh=fine,
        in_specs=(
            P(tm, tp, None, None),
            P(None, tm),
            P(),
            P(),
            P(None, tp),
            P(tp),
            P(None, tp),
            P(tp),
        ),
        out_specs=P(tm, None, None, tp),
        check_vma=False,
    )
```

```python
import jax
import jax.numpy as jnp
from jax import lax
from jax.experimental import pallas as pl
from jax.experimental.pallas import tpu as pltpu
from jax.sharding import Mesh, PartitionSpec as P

BF = jnp.bfloat16
F32 = jnp.float32
KP, C, HID = 1176, 1280, 5120
NX, NZ, NY = 4, 4, 8
PART = 320
TOK = 256
ORDER = (0, -1, -2, -3, -4, 1, 2, 3)


def shift(v, axis, n, by):
    return lax.ppermute(v, axis, [(i, (i + by) % n) for i in range(n)])


def shift_cores(v, by):
    def at(z, c):
        z = z % 8
        return ((z % 4) * 2 + z // 4) * 2 + c

    pairs = [(at(z, c), at(z + (by if c else -by), c)) for z in range(8) for c in range(2)]
    return lax.ppermute(v, ("zl", "zh", "c"), pairs)


def embed_kernel(px, *refs):
    w_here, w_near, w_near_o, w_two, w_two_o, p_own, p_oth, gain, beta, b_own, b_oth = refs[:11]
    out, xs, ws, ps, es, gs, bs, os, ts, sems = refs[11:]
    zl, core = lax.axis_index("zl"), lax.axis_index("c")
    loads = []

    def load(src, dst):
        loads.append(pltpu.make_async_copy(src, dst, sems.at[len(loads)]))
        loads[-1].start()

    half = NY // 2
    load(px.at[pl.ds(0, half)], xs.at[pl.ds(0, half)])
    load(w_here, ws.at[:, zl])
    load(w_near, ws.at[:, lax.rem(zl + 1 + 2 * core, NZ)])
    load(w_near_o, ws.at[:, lax.rem(zl + 3 - 2 * core, NZ)])
    load(w_two, ws.at[pl.ds(2 * core, 2), lax.rem(zl + 2, NZ)])
    load(w_two_o, ws.at[pl.ds(2 - 2 * core, 2), lax.rem(zl + 2, NZ)])
    now = len(loads)
    load(px.at[pl.ds(half, half)], xs.at[pl.ds(half, half)])
    load(p_own, ps.at[core])
    load(p_oth, ps.at[1 - core])
    for src, dst in ((gain, gs), (beta, bs), (b_own, os), (b_oth, ts)):
        load(src, dst)
    for c in loads[:now]:
        c.wait()
    w = ws[...].reshape(C, KP)
    dims = (((1,), (1,)), ((), ()))
    for part in range(2):
        if part == 1:
            loads[now].wait()
        ys = slice(part * half, (part + 1) * half)
        for ij in (0, 2):
            patches = [xs[ys, :, ij + n].reshape(TOK // 2, KP) for n in range(2)]
            patches = jnp.concatenate(patches, axis=0)
            e = lax.dot_general(patches, w, dims, preferred_element_type=F32)
            es[ij, part] = e[: TOK // 2]
            es[ij + 1, part] = e[TOK // 2 :]
    for c in loads[now + 1 :]:
        c.wait()
    g = gs[...].reshape(1, C)
    b = bs[...].reshape(1, C)
    p = ps[...].reshape(PART, HID)
    pre = None
    for ij in range(4):
        e = es[ij].reshape(TOK, C)
        mean = jnp.sum(e, axis=-1, keepdims=True) * (1.0 / C)
        cen = e - mean
        var = jnp.sum(cen * cen, axis=-1, keepdims=True) * (1.0 / C)
        normed = (cen * lax.rsqrt(var + 1e-06) * g + b).astype(BF)
        part = lax.dot_general(
            normed, p[:, ij * C : (ij + 1) * C], dims, preferred_element_type=F32
        )
        pre = part if ij == 0 else pre + part
    bias = [r[...].reshape(1, -1)[:, : PART // 2] for r in (os, ts)]
    bias = [jnp.where(core == n, bias[0], bias[1]) for n in range(2)]
    pre += jnp.concatenate(bias, axis=1)
    h = 0.5 * pre * (1.0 + lax.erf(pre * (0.5**0.5)))
    for y in range(NY):
        top = h[y * 32 : y * 32 + 16]
        low = h[y * 32 + 16 : y * 32 + 32]
        row = [top[:, :256], top[:, 256:], low[:, 256:], low[:, :256]]
        out[y] = jnp.concatenate(row, axis=1).astype(BF)


def embed_hidden(px, w, p_own, p_oth, gain, beta, b_own, b_oth):
    vmem = pl.BlockSpec(memory_space=pltpu.VMEM)
    any_ = pl.BlockSpec(memory_space=pl.ANY)
    out = pl.pallas_call(
        embed_kernel,
        out_shape=jax.ShapeDtypeStruct((NY, 16, 2 * PART), BF),
        in_specs=[any_] * 12,
        out_specs=vmem,
        scratch_shapes=[
            pltpu.VMEM((NY, 2, 4, 16, KP), BF),
            pltpu.VMEM((NX, NZ, 80, KP), BF),
            pltpu.VMEM((2, PART // 2, HID), BF),
            pltpu.VMEM((4, 2, TOK // 2, C), F32),
            pltpu.VMEM((C,), F32),
            pltpu.VMEM((C,), F32),
            pltpu.VMEM((160 + 256,), F32),
            pltpu.VMEM((160 + 256,), F32),
            pltpu.SemaphoreType.DMA((13,)),
        ],
        compiler_params=pltpu.CompilerParams(vmem_limit_bytes=56 << 20),
        cost_estimate=pl.CostEstimate(
            flops=2 * (1024 * KP * C + TOK * HID * PART), bytes_accessed=9 << 20, transcendentals=0
        ),
        name="embed_hidden",
    )(px, *w, p_own, p_oth, gain, beta, b_own, b_oth)
    return out.reshape(TOK // 2, 2 * PART)


def out_kernel(*refs):
    hs = refs[:NY]
    p_own, p_oth, b_own, b_oth, o_own, o_oth, hv, acc, bs, sems = refs[NY:]
    loads = [pltpu.make_async_copy(b, bs.at[n], sems.at[n]) for n, b in enumerate((b_own, b_oth))]
    for c in loads:
        c.start()
    y = lax.axis_index("y")
    for n, d in enumerate(ORDER):
        hv[lax.rem(y + (d + NY), NY)] = hs[n][...]
    lane = lax.broadcasted_iota(jnp.int32, (TOK // 2, 128), 1)
    for zh in range(2):
        for n in range(NY):
            row = (zh * NY + n) * PART
            h = hv[n, zh]
            both = jnp.concatenate([h[:, :256], h[:, 384:]], axis=0)
            mid = h[:, 256:384]
            low = jnp.where(lane >= 64, mid.astype(F32), 0.0).astype(BF)
            for k, p in enumerate((p_own, p_oth)):
                part = jnp.dot(both, p[row : row + 256, :], preferred_element_type=F32)
                rest = [
                    jnp.dot(mid[:, :64], p[row + 256 : row + 320, :], preferred_element_type=F32),
                    jnp.dot(low, p[row + 192 : row + 320, :], preferred_element_type=F32),
                ]
                part = part + jnp.concatenate(rest, axis=0)
                if row == 0:
                    acc[k] = part
                else:
                    acc[k] += part
    for k, o in enumerate((o_own, o_oth)):
        loads[k].wait()
        bias = bs[k : k + 1, PART // 2 :]
        o[...] = (acc[k] + bias).astype(BF)


def project_out(hs, p_own, p_oth, b_own, b_oth):
    any_ = pl.BlockSpec(memory_space=pl.ANY)
    vmem = pl.BlockSpec(memory_space=pltpu.VMEM)
    return pl.pallas_call(
        out_kernel,
        out_shape=[jax.ShapeDtypeStruct((TOK, 256), BF)] * 2,
        in_specs=[vmem] * 10 + [any_] * 2,
        out_specs=[vmem] * 2,
        scratch_shapes=[
            pltpu.VMEM((NY, 2, TOK // 2, 2 * PART), BF),
            pltpu.VMEM((2, TOK, 256), F32),
            pltpu.VMEM((2, 160 + 256), F32),
            pltpu.SemaphoreType.DMA((2,)),
        ],
        compiler_params=pltpu.CompilerParams(vmem_limit_bytes=12 << 20),
        cost_estimate=pl.CostEstimate(
            flops=2 * TOK * HID * 512, bytes_accessed=1 << 20, transcendentals=0
        ),
        name="project_out",
    )(*hs, p_own, p_oth, b_own, b_oth)


def ring(v):
    right, left = [v], [v]
    for step in range(4):
        right.append(shift(right[-1], "y", NY, 1))
        if step < 3:
            left.append(shift(left[-1], "y", NY, -1))
    return right + left[1:]


def per_device(pixels, conv_weight, norm_gain, norm_bias, proj_in, bias_in, proj_out, bias_out):
    core = lax.axis_index("c")
    first = core == 0

    rows = lax.all_gather(pixels.reshape(2, 32, KP), ("zh", "c"), axis=0).reshape(2, 2, 2, 32, KP)
    rows = jnp.where(first, rows[:, :, 0], rows[:, :, 1])
    half = rows.reshape(2, 2, 16, 2, KP).transpose(0, 1, 3, 2, 4).reshape(2, 4, 16, KP)
    px = lax.all_gather(half, "y", axis=0)

    wt, _ = lax.optimization_barrier((conv_weight.T, half))
    wx = lax.all_gather(wt, "x", axis=0)

    near = shift_cores(wx, 1)
    part = jnp.where(first, wx[: NX // 2], wx[NX // 2 :])
    two = shift_cores(part, 2)
    near, two = lax.optimization_barrier((near, two))
    near_o = shift(near, "c", 2, 1)
    two_o = shift(two, "c", 2, 1)

    bias = jnp.concatenate([bias_in, bias_out])
    p_in, p_out, bias, _ = lax.optimization_barrier((proj_in.T, proj_out, bias, part))
    p_in_o, p_out_o, bias_o = [shift(v, "c", 2, 1) for v in (p_in, p_out, bias)]
    hid = embed_hidden(
        px,
        (wx, near, near_o, two, two_o),
        p_in,
        p_in_o,
        norm_gain,
        norm_bias,
        bias,
        bias_o,
    )
    hs = ring(lax.all_gather(hid, "zh", axis=0))
    o_own, o_oth = project_out(hs, p_out, p_out_o, bias, bias_o)
    o_got = shift(o_oth, "c", 2, 1)
    result = jnp.stack([jnp.where(first, o_own, o_got), jnp.where(first, o_got, o_own)])
    return result.reshape(2, 16, 16, 256)


def solution(mesh):
    fine = Mesh(mesh.devices.reshape(NX, NZ, 2, NY, 2), ("x", "zl", "zh", "y", "c"))
    tm, tp = ("x", "zl"), ("zh", "y", "c")
    return jax.shard_map(
        per_device,
        mesh=fine,
        in_specs=(
            P(tm, tp, None, None),
            P(None, tm),
            P(),
            P(),
            P(None, tp),
            P(tp),
            P(None, tp),
            P(tp),
        ),
        out_specs=P(tm, None, None, tp),
        check_vma=False,
    )
```

```python
import jax
import jax.numpy as jnp
from jax import lax
from jax.experimental import pallas as pl
from jax.experimental.pallas import tpu as pltpu
from jax.sharding import Mesh, PartitionSpec as P

BF = jnp.bfloat16
F32 = jnp.float32
KP, C, HID = 1176, 1280, 5120
NX, NZ, NY = 4, 4, 8
PART = 320
TOK = 256
ORDER = (0, -1, -2, -3, 1, 2, 3, -4)


def shift(v, axis, n, by):
    return lax.ppermute(v, axis, [(i, (i + by) % n) for i in range(n)])


def shift_cores(v, by):
    def at(z, c):
        z = z % 8
        return ((z % 4) * 2 + z // 4) * 2 + c

    pairs = [(at(z, c), at(z + (by if c else -by), c)) for z in range(8) for c in range(2)]
    return lax.ppermute(v, ("zl", "zh", "c"), pairs)


def embed_kernel(px, *refs):
    w_here, w_near, w_near_o, w_two, w_two_o, p_own, p_oth, gain, beta, b_own, b_oth = refs[:11]
    out, xs, ws, ps, es, gs, bs, os, ts, sems = refs[11:]
    zl, core = lax.axis_index("zl"), lax.axis_index("c")
    loads = []

    def load(src, dst):
        loads.append(pltpu.make_async_copy(src, dst, sems.at[len(loads)]))
        loads[-1].start()

    half = NY // 2
    load(px.at[pl.ds(0, half)], xs.at[pl.ds(0, half)])
    load(w_here, ws.at[:, zl])
    load(w_near, ws.at[:, lax.rem(zl + 1 + 2 * core, NZ)])
    load(w_near_o, ws.at[:, lax.rem(zl + 3 - 2 * core, NZ)])
    load(w_two, ws.at[pl.ds(2 * core, 2), lax.rem(zl + 2, NZ)])
    load(w_two_o, ws.at[pl.ds(2 - 2 * core, 2), lax.rem(zl + 2, NZ)])
    now = len(loads)
    load(px.at[pl.ds(half, half)], xs.at[pl.ds(half, half)])
    load(p_own, ps.at[core])
    load(p_oth, ps.at[1 - core])
    for src, dst in ((gain, gs), (beta, bs), (b_own, os), (b_oth, ts)):
        load(src, dst)
    for c in loads[:now]:
        c.wait()
    w = ws[...].reshape(C, KP)
    dims = (((1,), (1,)), ((), ()))
    for part in range(2):
        if part == 1:
            loads[now].wait()
        ys = slice(part * half, (part + 1) * half)
        for ij in (0, 2):
            patches = [xs[ys, :, ij + n].reshape(TOK // 2, KP) for n in range(2)]
            patches = jnp.concatenate(patches, axis=0)
            e = lax.dot_general(patches, w, dims, preferred_element_type=F32)
            es[ij, part] = e[: TOK // 2]
            es[ij + 1, part] = e[TOK // 2 :]
    for c in loads[now + 1 :]:
        c.wait()
    g = gs[...].reshape(1, C)
    b = bs[...].reshape(1, C)
    p = ps[...].reshape(PART, HID)
    pre = None
    for ij in range(4):
        e = es[ij].reshape(TOK, C)
        mean = jnp.sum(e, axis=-1, keepdims=True) * (1.0 / C)
        cen = e - mean
        var = jnp.sum(cen * cen, axis=-1, keepdims=True) * (1.0 / C)
        normed = (cen * lax.rsqrt(var + 1e-06) * g + b).astype(BF)
        part = lax.dot_general(
            normed, p[:, ij * C : (ij + 1) * C], dims, preferred_element_type=F32
        )
        pre = part if ij == 0 else pre + part
    bias = [r[...].reshape(1, -1)[:, : PART // 2] for r in (os, ts)]
    bias = [jnp.where(core == n, bias[0], bias[1]) for n in range(2)]
    pre += jnp.concatenate(bias, axis=1)
    h = 0.5 * pre * (1.0 + lax.erf(pre * (0.5**0.5)))
    for y in range(NY):
        top = h[y * 32 : y * 32 + 16]
        low = h[y * 32 + 16 : y * 32 + 32]
        row = [top[:, :256], top[:, 256:], low[:, 256:], low[:, :256]]
        out[y] = jnp.concatenate(row, axis=1).astype(BF)


def embed_hidden(px, w, p_own, p_oth, gain, beta, b_own, b_oth):
    vmem = pl.BlockSpec(memory_space=pltpu.VMEM)
    any_ = pl.BlockSpec(memory_space=pl.ANY)
    out = pl.pallas_call(
        embed_kernel,
        out_shape=jax.ShapeDtypeStruct((NY, 16, 2 * PART), BF),
        in_specs=[any_] * 12,
        out_specs=vmem,
        scratch_shapes=[
            pltpu.VMEM((NY, 2, 4, 16, KP), BF),
            pltpu.VMEM((NX, NZ, 80, KP), BF),
            pltpu.VMEM((2, PART // 2, HID), BF),
            pltpu.VMEM((4, 2, TOK // 2, C), F32),
            pltpu.VMEM((C,), F32),
            pltpu.VMEM((C,), F32),
            pltpu.VMEM((160 + 256,), F32),
            pltpu.VMEM((160 + 256,), F32),
            pltpu.SemaphoreType.DMA((13,)),
        ],
        compiler_params=pltpu.CompilerParams(vmem_limit_bytes=60 << 20),
        cost_estimate=pl.CostEstimate(
            flops=2 * (1024 * KP * C + TOK * HID * PART), bytes_accessed=9 << 20, transcendentals=0
        ),
        name="embed_hidden",
    )(px, *w, p_own, p_oth, gain, beta, b_own, b_oth)
    return out.reshape(TOK // 2, 2 * PART)


def hidden_dot(h, lane, w):
    both = jnp.concatenate([h[:, :256], h[:, 384:]], axis=0)
    mid = h[:, 256:384]
    low = jnp.where(lane >= 64, mid.astype(F32), 0.0).astype(BF)
    rest = [
        jnp.dot(mid[:, :64], w(256, 320), preferred_element_type=F32),
        jnp.dot(low, w(192, 320), preferred_element_type=F32),
    ]
    return jnp.dot(both, w(0, 256), preferred_element_type=F32) + jnp.concatenate(rest, axis=0)


def most_kernel(*refs):
    hs = refs[: NY - 1]
    p_own, p_oth, b_own, b_oth, acc, far, hv, bs, sems = refs[NY - 1 :]
    y = lax.axis_index("y")
    loads = [pltpu.make_async_copy(b, bs.at[n], sems.at[n]) for n, b in enumerate((b_own, b_oth))]
    last = lax.rem(y + NY // 2, NY)
    for k, p in enumerate((p_own, p_oth)):
        for zh in range(2):
            rows = pl.ds(pl.multiple_of((zh * NY + last) * PART, 64), PART)
            loads.append(pltpu.make_async_copy(p.at[rows], far.at[k, zh], sems.at[2 + 2 * k + zh]))
    for c in loads:
        c.start()
    hv[last] = jnp.zeros_like(hs[0])
    for n, d in enumerate(ORDER[:-1]):
        hv[lax.rem(y + (d + NY), NY)] = hs[n][...]
    lane = lax.broadcasted_iota(jnp.int32, (TOK // 2, 128), 1)
    for zh in range(2):
        for n in range(NY):
            row = (zh * NY + n) * PART
            h = hv[n, zh]
            for k, p in enumerate((p_own, p_oth)):
                part = hidden_dot(h, lane, lambda a, b: p[row + a : row + b, :])
                if row == 0:
                    acc[k] = part
                else:
                    acc[k] += part
    for c in loads:
        c.wait()
    for k in range(2):
        acc[k] += bs[k : k + 1, PART // 2 :]


def last_kernel(h, acc, far, o_own, o_oth):
    lane = lax.broadcasted_iota(jnp.int32, (TOK // 2, 128), 1)
    for k, o in enumerate((o_own, o_oth)):
        total = acc[k]
        for zh in range(2):
            total += hidden_dot(h[zh], lane, lambda a, b: far[k, zh, a:b, :])
        o[...] = total.astype(BF)


def project_out(hs, p_own, p_oth, b_own, b_oth):
    any_ = pl.BlockSpec(memory_space=pl.ANY)
    vmem = pl.BlockSpec(memory_space=pltpu.VMEM)
    acc, far = pl.pallas_call(
        most_kernel,
        out_shape=[
            jax.ShapeDtypeStruct((2, TOK, 256), F32),
            jax.ShapeDtypeStruct((2, 2, PART, 256), BF),
        ],
        in_specs=[vmem] * 9 + [any_] * 2,
        out_specs=[vmem] * 2,
        scratch_shapes=[
            pltpu.VMEM((NY, 2, TOK // 2, 2 * PART), BF),
            pltpu.VMEM((2, 160 + 256), F32),
            pltpu.SemaphoreType.DMA((6,)),
        ],
        compiler_params=pltpu.CompilerParams(vmem_limit_bytes=12 << 20),
        cost_estimate=pl.CostEstimate(
            flops=2 * TOK * HID * 512, bytes_accessed=1 << 20, transcendentals=0
        ),
        name="project_most",
    )(*hs[:-1], p_own, p_oth, b_own, b_oth)
    return pl.pallas_call(
        last_kernel,
        out_shape=[jax.ShapeDtypeStruct((TOK, 256), BF)] * 2,
        in_specs=[vmem] * 3,
        out_specs=[vmem] * 2,
        compiler_params=pltpu.CompilerParams(vmem_limit_bytes=8 << 20),
        cost_estimate=pl.CostEstimate(
            flops=2 * TOK * 2 * PART * 512, bytes_accessed=1 << 18, transcendentals=0
        ),
        name="project_last",
    )(hs[-1], acc, far)


def ring(v):
    right, left = [v], [v]
    for step in range(4):
        right.append(shift(right[-1], "y", NY, 1))
        if step < 3:
            left.append(shift(left[-1], "y", NY, -1))
    return right[:4] + left[1:] + right[4:]


def per_device(pixels, conv_weight, norm_gain, norm_bias, proj_in, bias_in, proj_out, bias_out):
    core = lax.axis_index("c")
    first = core == 0

    rows = lax.all_gather(pixels.reshape(2, 32, KP), ("zh", "c"), axis=0).reshape(2, 2, 2, 32, KP)
    rows = jnp.where(first, rows[:, :, 0], rows[:, :, 1])
    half = rows.reshape(2, 2, 16, 2, KP).transpose(0, 1, 3, 2, 4).reshape(2, 4, 16, KP)
    px = lax.all_gather(half, "y", axis=0)

    wt, _ = lax.optimization_barrier((conv_weight.T, half))
    wx = lax.all_gather(wt, "x", axis=0)

    near = shift_cores(wx, 1)
    part = jnp.where(first, wx[: NX // 2], wx[NX // 2 :])
    two = shift_cores(part, 2)
    bias = jnp.concatenate([bias_in, bias_out])
    p_in, p_out, bias, _ = lax.optimization_barrier((proj_in.T, proj_out, bias, part))
    p_in_o, p_out_o, bias_o = [shift(v, "c", 2, 1) for v in (p_in, p_out, bias)]
    near, two, bias_o = lax.optimization_barrier((near, two, bias_o))
    near_o = shift(near, "c", 2, 1)
    two_o = shift(two, "c", 2, 1)
    hid = embed_hidden(
        px,
        (wx, near, near_o, two, two_o),
        p_in,
        p_in_o,
        norm_gain,
        norm_bias,
        bias,
        bias_o,
    )
    hs = ring(lax.all_gather(hid, "zh", axis=0))
    o_own, o_oth = project_out(hs, p_out, p_out_o, bias, bias_o)
    o_got = lax.all_gather(o_oth, "c", axis=0)
    result = jnp.stack([jnp.where(first, o_own, o_got[0]), jnp.where(first, o_got[1], o_own)])
    return result.reshape(2, 16, 16, 256)


def solution(mesh):
    fine = Mesh(mesh.devices.reshape(NX, NZ, 2, NY, 2), ("x", "zl", "zh", "y", "c"))
    tm, tp = ("x", "zl"), ("zh", "y", "c")
    return jax.shard_map(
        per_device,
        mesh=fine,
        in_specs=(
            P(tm, tp, None, None),
            P(None, tm),
            P(),
            P(),
            P(None, tp),
            P(tp),
            P(None, tp),
            P(tp),
        ),
        out_specs=P(tm, None, None, tp),
        check_vma=False,
    )
```

```python
import jax
import jax.numpy as jnp
from jax import lax
from jax.experimental import pallas as pl
from jax.experimental.pallas import tpu as pltpu
from jax.sharding import Mesh, PartitionSpec as P

BF = jnp.bfloat16
F32 = jnp.float32
KP, C, HID = 1176, 1280, 5120
NX, NZ, NY = 4, 4, 8
PART = 320
TOK = 256
ORDER = (0, -1, -2, -3, 1, 2, 3, -4)


def shift(v, axis, n, by):
    return lax.ppermute(v, axis, [(i, (i + by) % n) for i in range(n)])


def shift_cores(v, by):
    def at(z, c):
        z = z % 8
        return ((z % 4) * 2 + z // 4) * 2 + c

    pairs = [(at(z, c), at(z + (by if c else -by), c)) for z in range(8) for c in range(2)]
    return lax.ppermute(v, ("zl", "zh", "c"), pairs)


def embed_kernel(px, *refs):
    w_here, w_near, w_near_o, w_two, w_two_o, p_own, p_oth, gain, beta, b_own, b_oth = refs[:11]
    out, xs, ws, ps, es, gs, bs, os, ts, sems = refs[11:]
    zl, core = lax.axis_index("zl"), lax.axis_index("c")
    loads = []

    def load(src, dst):
        loads.append(pltpu.make_async_copy(src, dst, sems.at[len(loads)]))
        loads[-1].start()

    half = NY // 2
    load(px.at[pl.ds(0, half)], xs.at[pl.ds(0, half)])
    load(w_here, ws.at[:, zl])
    load(w_near, ws.at[:, lax.rem(zl + 1 + 2 * core, NZ)])
    load(w_near_o, ws.at[:, lax.rem(zl + 3 - 2 * core, NZ)])
    load(w_two, ws.at[pl.ds(2 * core, 2), lax.rem(zl + 2, NZ)])
    load(w_two_o, ws.at[pl.ds(2 - 2 * core, 2), lax.rem(zl + 2, NZ)])
    now = len(loads)
    load(px.at[pl.ds(half, half)], xs.at[pl.ds(half, half)])
    load(p_own, ps.at[core])
    load(p_oth, ps.at[1 - core])
    for src, dst in ((gain, gs), (beta, bs), (b_own, os), (b_oth, ts)):
        load(src, dst)
    for c in loads[:now]:
        c.wait()
    w = ws[...].reshape(C, KP)
    dims = (((1,), (1,)), ((), ()))
    for part in range(2):
        if part == 1:
            loads[now].wait()
        ys = slice(part * half, (part + 1) * half)
        for ij in (0, 2):
            patches = [xs[ys, :, ij + n].reshape(TOK // 2, KP) for n in range(2)]
            patches = jnp.concatenate(patches, axis=0)
            e = lax.dot_general(patches, w, dims, preferred_element_type=F32)
            es[ij, part] = e[: TOK // 2]
            es[ij + 1, part] = e[TOK // 2 :]
    for c in loads[now + 1 :]:
        c.wait()
    g = gs[...].reshape(1, C)
    b = bs[...].reshape(1, C)
    p = ps[...].reshape(PART, HID)
    pre = None
    for ij in range(4):
        e = es[ij].reshape(TOK, C)
        mean = jnp.sum(e, axis=-1, keepdims=True) * (1.0 / C)
        cen = e - mean
        var = jnp.sum(cen * cen, axis=-1, keepdims=True) * (1.0 / C)
        normed = (cen * lax.rsqrt(var + 1e-06) * g + b).astype(BF)
        part = lax.dot_general(
            normed, p[:, ij * C : (ij + 1) * C], dims, preferred_element_type=F32
        )
        pre = part if ij == 0 else pre + part
    bias = [r[...].reshape(1, -1)[:, : PART // 2] for r in (os, ts)]
    bias = [jnp.where(core == n, bias[0], bias[1]) for n in range(2)]
    pre += jnp.concatenate(bias, axis=1)
    h = 0.5 * pre * (1.0 + lax.erf(pre * (0.5**0.5)))
    for y in range(NY):
        top = h[y * 32 : y * 32 + 16]
        low = h[y * 32 + 16 : y * 32 + 32]
        row = [top[:, :256], top[:, 256:], low[:, 256:], low[:, :256]]
        out[y] = jnp.concatenate(row, axis=1).astype(BF)


def embed_hidden(px, w, p_own, p_oth, gain, beta, b_own, b_oth):
    vmem = pl.BlockSpec(memory_space=pltpu.VMEM)
    any_ = pl.BlockSpec(memory_space=pl.ANY)
    out = pl.pallas_call(
        embed_kernel,
        out_shape=jax.ShapeDtypeStruct((NY, 16, 2 * PART), BF),
        in_specs=[any_] * 12,
        out_specs=vmem,
        scratch_shapes=[
            pltpu.VMEM((NY, 2, 4, 16, KP), BF),
            pltpu.VMEM((NX, NZ, 80, KP), BF),
            pltpu.VMEM((2, PART // 2, HID), BF),
            pltpu.VMEM((4, 2, TOK // 2, C), F32),
            pltpu.VMEM((C,), F32),
            pltpu.VMEM((C,), F32),
            pltpu.VMEM((160 + 256,), F32),
            pltpu.VMEM((160 + 256,), F32),
            pltpu.SemaphoreType.DMA((13,)),
        ],
        compiler_params=pltpu.CompilerParams(vmem_limit_bytes=60 << 20),
        cost_estimate=pl.CostEstimate(
            flops=2 * (1024 * KP * C + TOK * HID * PART), bytes_accessed=9 << 20, transcendentals=0
        ),
        name="embed_hidden",
    )(px, *w, p_own, p_oth, gain, beta, b_own, b_oth)
    return out.reshape(TOK // 2, 2 * PART)


def hidden_dot(h, lane, w):
    both = jnp.concatenate([h[:, :256], h[:, 384:]], axis=0)
    mid = h[:, 256:384]
    low = jnp.where(lane >= 64, mid.astype(F32), 0.0).astype(BF)
    rest = [
        jnp.dot(mid[:, :64], w(256, 320), preferred_element_type=F32),
        jnp.dot(low, w(192, 320), preferred_element_type=F32),
    ]
    return jnp.dot(both, w(0, 256), preferred_element_type=F32) + jnp.concatenate(rest, axis=0)


def most_kernel(*refs):
    hs = refs[: NY - 1]
    p_own, p_oth, b_own, b_oth, acc, far, hv, bs, sems = refs[NY - 1 :]
    y = lax.axis_index("y")
    loads = [pltpu.make_async_copy(b, bs.at[n], sems.at[n]) for n, b in enumerate((b_own, b_oth))]
    last = lax.rem(y + NY // 2, NY)
    for k, p in enumerate((p_own, p_oth)):
        for zh in range(2):
            rows = pl.ds(pl.multiple_of((zh * NY + last) * PART, 64), PART)
            loads.append(pltpu.make_async_copy(p.at[rows], far.at[k, zh], sems.at[2 + 2 * k + zh]))
    for c in loads:
        c.start()
    hv[last] = jnp.zeros_like(hs[0])
    for n, d in enumerate(ORDER[:-1]):
        hv[lax.rem(y + (d + NY), NY)] = hs[n][...]
    lane = lax.broadcasted_iota(jnp.int32, (TOK // 2, 128), 1)
    for zh in range(2):
        for n in range(NY):
            row = (zh * NY + n) * PART
            h = hv[n, zh]
            for k, p in enumerate((p_own, p_oth)):
                part = hidden_dot(h, lane, lambda a, b: p[row + a : row + b, :])
                if row == 0:
                    acc[k] = part
                else:
                    acc[k] += part
    for c in loads:
        c.wait()
    for k in range(2):
        acc[k] += bs[k : k + 1, PART // 2 :]


def last_kernel(h, acc, far, o_own, o_oth):
    lane = lax.broadcasted_iota(jnp.int32, (TOK // 2, 128), 1)
    for k, o in enumerate((o_own, o_oth)):
        total = acc[k]
        for zh in range(2):
            total += hidden_dot(h[zh], lane, lambda a, b: far[k, zh, a:b, :])
        o[...] = total.astype(BF)


def project_out(hs, p_own, p_oth, b_own, b_oth):
    any_ = pl.BlockSpec(memory_space=pl.ANY)
    vmem = pl.BlockSpec(memory_space=pltpu.VMEM)
    acc, far = pl.pallas_call(
        most_kernel,
        out_shape=[
            jax.ShapeDtypeStruct((2, TOK, 256), F32),
            jax.ShapeDtypeStruct((2, 2, PART, 256), BF),
        ],
        in_specs=[vmem] * 9 + [any_] * 2,
        out_specs=[vmem] * 2,
        scratch_shapes=[
            pltpu.VMEM((NY, 2, TOK // 2, 2 * PART), BF),
            pltpu.VMEM((2, 160 + 256), F32),
            pltpu.SemaphoreType.DMA((6,)),
        ],
        compiler_params=pltpu.CompilerParams(vmem_limit_bytes=12 << 20),
        cost_estimate=pl.CostEstimate(
            flops=2 * TOK * HID * 512, bytes_accessed=1 << 20, transcendentals=0
        ),
        name="project_most",
    )(*hs[:-1], p_own, p_oth, b_own, b_oth)
    return pl.pallas_call(
        last_kernel,
        out_shape=[jax.ShapeDtypeStruct((TOK, 256), BF)] * 2,
        in_specs=[vmem] * 3,
        out_specs=[vmem] * 2,
        compiler_params=pltpu.CompilerParams(vmem_limit_bytes=8 << 20),
        cost_estimate=pl.CostEstimate(
            flops=2 * TOK * 2 * PART * 512, bytes_accessed=1 << 18, transcendentals=0
        ),
        name="project_last",
    )(hs[-1], acc, far)


def ring(v):
    right, left = [v], [v]
    for step in range(4):
        right.append(shift(right[-1], "y", NY, 1))
        if step < 3:
            left.append(shift(left[-1], "y", NY, -1))
    return right[:4] + left[1:] + right[4:]


def per_device(pixels, conv_weight, norm_gain, norm_bias, proj_in, bias_in, proj_out, bias_out):
    core = lax.axis_index("c")
    first = core == 0

    rows = lax.all_gather(pixels.reshape(2, 32, KP), ("zh", "c"), axis=0).reshape(2, 2, 2, 32, KP)
    rows = jnp.where(first, rows[:, :, 0], rows[:, :, 1])
    half = rows.reshape(2, 2, 16, 2, KP).transpose(0, 1, 3, 2, 4).reshape(2, 4, 16, KP)
    px = lax.all_gather(half, "y", axis=0)

    wt, _ = lax.optimization_barrier((conv_weight.T, half))
    wx = lax.all_gather(wt, "x", axis=0)

    near = shift_cores(wx, 1)
    part = jnp.where(first, wx[: NX // 2], wx[NX // 2 :])
    two = shift_cores(part, 2)
    bias = jnp.concatenate([bias_in, bias_out])
    p_in, p_out, bias, _ = lax.optimization_barrier((proj_in.T, proj_out, bias, part))
    p_in_o, p_out_o, bias_o = [shift(v, "c", 2, 1) for v in (p_in, p_out, bias)]
    near_o = shift(near, "c", 2, 1)
    two, bias_o = lax.optimization_barrier((two, bias_o))
    two_o = shift(two, "c", 2, 1)
    hid = embed_hidden(
        px,
        (wx, near, near_o, two, two_o),
        p_in,
        p_in_o,
        norm_gain,
        norm_bias,
        bias,
        bias_o,
    )
    hs = ring(lax.all_gather(hid, "zh", axis=0))
    o_own, o_oth = project_out(hs, p_out, p_out_o, bias, bias_o)
    o_got = lax.all_gather(o_oth, "c", axis=0)
    result = jnp.stack([jnp.where(first, o_own, o_got[0]), jnp.where(first, o_got[1], o_own)])
    return result.reshape(2, 16, 16, 256)


def solution(mesh):
    fine = Mesh(mesh.devices.reshape(NX, NZ, 2, NY, 2), ("x", "zl", "zh", "y", "c"))
    tm, tp = ("x", "zl"), ("zh", "y", "c")
    return jax.shard_map(
        per_device,
        mesh=fine,
        in_specs=(
            P(tm, tp, None, None),
            P(None, tm),
            P(),
            P(),
            P(None, tp),
            P(tp),
            P(None, tp),
            P(tp),
        ),
        out_specs=P(tm, None, None, tp),
        check_vma=False,
    )
```

```python
import jax
import jax.numpy as jnp
from jax import lax
from jax.experimental import pallas as pl
from jax.experimental.pallas import tpu as pltpu
from jax.sharding import Mesh, PartitionSpec as P

BF = jnp.bfloat16
F32 = jnp.float32
KP, C, HID = 1176, 1280, 5120
NX, NZ, NY = 4, 4, 8
PART = 320
TOK = 256
ORDER = (0, -1, -2, -3, 1, 2, 3, -4)


def shift(v, axis, n, by):
    return lax.ppermute(v, axis, [(i, (i + by) % n) for i in range(n)])


def shift_cores(v, by):
    def at(z, c):
        z = z % 8
        return ((z % 4) * 2 + z // 4) * 2 + c

    pairs = [(at(z, c), at(z + (by if c else -by), c)) for z in range(8) for c in range(2)]
    return lax.ppermute(v, ("zl", "zh", "c"), pairs)


def embed_kernel(px, *refs):
    w_here, w_near, w_near_o, w_two, w_two_o, p_own, p_oth, gain, beta, b_own, b_oth = refs[:11]
    out, later, xs, ws, ps, es, gs, bs, os, ts, sems = refs[11:]
    zl, core = lax.axis_index("zl"), lax.axis_index("c")
    loads = []

    def load(src, dst):
        loads.append(pltpu.make_async_copy(src, dst, sems.at[len(loads)]))
        loads[-1].start()

    half = NY // 2
    load(px.at[pl.ds(0, half)], xs.at[pl.ds(0, half)])
    load(w_here, ws.at[:, zl])
    load(w_near, ws.at[:, lax.rem(zl + 1 + 2 * core, NZ)])
    load(w_near_o, ws.at[:, lax.rem(zl + 3 - 2 * core, NZ)])
    load(w_two, ws.at[pl.ds(2 * core, 2), lax.rem(zl + 2, NZ)])
    load(w_two_o, ws.at[pl.ds(2 - 2 * core, 2), lax.rem(zl + 2, NZ)])
    now = len(loads)
    load(px.at[pl.ds(half, half)], xs.at[pl.ds(half, half)])
    load(p_own, ps.at[core])
    load(p_oth, ps.at[1 - core])
    for src, dst in ((gain, gs), (beta, bs), (b_own, os), (b_oth, ts)):
        load(src, dst)
    for c in loads[:now]:
        c.wait()
    w = ws[...].reshape(C, KP)
    dims = (((1,), (1,)), ((), ()))
    for part in range(2):
        if part == 1:
            loads[now].wait()
        ys = slice(part * half, (part + 1) * half)
        for ij in (0, 2):
            patches = [xs[ys, :, ij + n].reshape(TOK // 2, KP) for n in range(2)]
            patches = jnp.concatenate(patches, axis=0)
            e = lax.dot_general(patches, w, dims, preferred_element_type=F32)
            es[ij, part] = e[: TOK // 2]
            es[ij + 1, part] = e[TOK // 2 :]
    for c in loads[now + 1 :]:
        c.wait()
    g = gs[...].reshape(1, C)
    b = bs[...].reshape(1, C)
    p = ps[...].reshape(PART, HID)
    pre = None
    for ij in range(4):
        e = es[ij].reshape(TOK, C)
        mean = jnp.sum(e, axis=-1, keepdims=True) * (1.0 / C)
        cen = e - mean
        var = jnp.sum(cen * cen, axis=-1, keepdims=True) * (1.0 / C)
        normed = (cen * lax.rsqrt(var + 1e-06) * g + b).astype(BF)
        part = lax.dot_general(
            normed, p[:, ij * C : (ij + 1) * C], dims, preferred_element_type=F32
        )
        pre = part if ij == 0 else pre + part
    bias = [r[...].reshape(1, -1) for r in (os, ts)]
    for n in range(2):
        later[n : n + 1, :] = bias[n][:, PART // 2 :]
    bias = [r[:, : PART // 2] for r in bias]
    bias = [jnp.where(core == n, bias[0], bias[1]) for n in range(2)]
    pre += jnp.concatenate(bias, axis=1)
    h = 0.5 * pre * (1.0 + lax.erf(pre * (0.5**0.5)))
    for y in range(NY):
        top = h[y * 32 : y * 32 + 16]
        low = h[y * 32 + 16 : y * 32 + 32]
        row = [top[:, :256], top[:, 256:], low[:, 256:], low[:, :256]]
        out[y] = jnp.concatenate(row, axis=1).astype(BF)


def embed_hidden(px, w, p_own, p_oth, gain, beta, b_own, b_oth):
    vmem = pl.BlockSpec(memory_space=pltpu.VMEM)
    any_ = pl.BlockSpec(memory_space=pl.ANY)
    out, later = pl.pallas_call(
        embed_kernel,
        out_shape=[
            jax.ShapeDtypeStruct((NY, 16, 2 * PART), BF),
            jax.ShapeDtypeStruct((2, 256), F32),
        ],
        in_specs=[any_] * 12,
        out_specs=[vmem] * 2,
        scratch_shapes=[
            pltpu.VMEM((NY, 2, 4, 16, KP), BF),
            pltpu.VMEM((NX, NZ, 80, KP), BF),
            pltpu.VMEM((2, PART // 2, HID), BF),
            pltpu.VMEM((4, 2, TOK // 2, C), F32),
            pltpu.VMEM((C,), F32),
            pltpu.VMEM((C,), F32),
            pltpu.VMEM((160 + 256,), F32),
            pltpu.VMEM((160 + 256,), F32),
            pltpu.SemaphoreType.DMA((13,)),
        ],
        compiler_params=pltpu.CompilerParams(vmem_limit_bytes=60 << 20),
        cost_estimate=pl.CostEstimate(
            flops=2 * (1024 * KP * C + TOK * HID * PART), bytes_accessed=9 << 20, transcendentals=0
        ),
        name="embed_hidden",
    )(px, *w, p_own, p_oth, gain, beta, b_own, b_oth)
    return out.reshape(TOK // 2, 2 * PART), later


def hidden_dot(h, lane, w):
    both = jnp.concatenate([h[:, :256], h[:, 384:]], axis=0)
    mid = h[:, 256:384]
    low = jnp.where(lane >= 64, mid.astype(F32), 0.0).astype(BF)
    rest = [
        jnp.dot(mid[:, :64], w(256, 320), preferred_element_type=F32),
        jnp.dot(low, w(192, 320), preferred_element_type=F32),
    ]
    return jnp.dot(both, w(0, 256), preferred_element_type=F32) + jnp.concatenate(rest, axis=0)


def most_kernel(*refs):
    hs = refs[: NY - 1]
    p_own, p_oth, bs, acc, far, hv, sems = refs[NY - 1 :]
    y = lax.axis_index("y")
    loads = []
    last = lax.rem(y + NY // 2, NY)
    for k, p in enumerate((p_own, p_oth)):
        for zh in range(2):
            rows = pl.ds(pl.multiple_of((zh * NY + last) * PART, 64), PART)
            loads.append(pltpu.make_async_copy(p.at[rows], far.at[k, zh], sems.at[2 * k + zh]))
    for c in loads:
        c.start()
    hv[last] = jnp.zeros_like(hs[0])
    for n, d in enumerate(ORDER[:-1]):
        hv[lax.rem(y + (d + NY), NY)] = hs[n][...]
    lane = lax.broadcasted_iota(jnp.int32, (TOK // 2, 128), 1)
    for zh in range(2):
        for n in range(NY):
            row = (zh * NY + n) * PART
            h = hv[n, zh]
            for k, p in enumerate((p_own, p_oth)):
                part = hidden_dot(h, lane, lambda a, b: p[row + a : row + b, :])
                if row == 0:
                    acc[k] = part
                else:
                    acc[k] += part
    for c in loads:
        c.wait()
    for k in range(2):
        acc[k] += bs[k : k + 1, :]


def last_kernel(h, acc, far, o_own, o_oth):
    lane = lax.broadcasted_iota(jnp.int32, (TOK // 2, 128), 1)
    for k, o in enumerate((o_own, o_oth)):
        total = acc[k]
        for zh in range(2):
            total += hidden_dot(h[zh], lane, lambda a, b: far[k, zh, a:b, :])
        o[...] = total.astype(BF)


def project_out(hs, p_own, p_oth, bias):
    vmem = pl.BlockSpec(memory_space=pltpu.VMEM)
    acc, far = pl.pallas_call(
        most_kernel,
        out_shape=[
            jax.ShapeDtypeStruct((2, TOK, 256), F32),
            jax.ShapeDtypeStruct((2, 2, PART, 256), BF),
        ],
        in_specs=[vmem] * 10,
        out_specs=[vmem] * 2,
        scratch_shapes=[
            pltpu.VMEM((NY, 2, TOK // 2, 2 * PART), BF),
            pltpu.SemaphoreType.DMA((4,)),
        ],
        compiler_params=pltpu.CompilerParams(vmem_limit_bytes=12 << 20),
        cost_estimate=pl.CostEstimate(
            flops=2 * TOK * HID * 512, bytes_accessed=1 << 20, transcendentals=0
        ),
        name="project_most",
    )(*hs[:-1], p_own, p_oth, bias)
    return pl.pallas_call(
        last_kernel,
        out_shape=[jax.ShapeDtypeStruct((TOK, 256), BF)] * 2,
        in_specs=[vmem] * 3,
        out_specs=[vmem] * 2,
        compiler_params=pltpu.CompilerParams(vmem_limit_bytes=8 << 20),
        cost_estimate=pl.CostEstimate(
            flops=2 * TOK * 2 * PART * 512, bytes_accessed=1 << 18, transcendentals=0
        ),
        name="project_last",
    )(hs[-1], acc, far)


def ring(v):
    right, left = [v], [v]
    for step in range(4):
        right.append(shift(right[-1], "y", NY, 1))
        if step < 3:
            left.append(shift(left[-1], "y", NY, -1))
    return right[:4] + left[1:] + right[4:]


def per_device(pixels, conv_weight, norm_gain, norm_bias, proj_in, bias_in, proj_out, bias_out):
    core = lax.axis_index("c")
    first = core == 0

    rows = lax.all_gather(pixels.reshape(2, 32, KP), ("zh", "c"), axis=0).reshape(2, 2, 2, 32, KP)
    rows = jnp.where(first, rows[:, :, 0], rows[:, :, 1])
    half = rows.reshape(2, 2, 16, 2, KP).transpose(0, 1, 3, 2, 4).reshape(2, 4, 16, KP)
    px = lax.all_gather(half, "y", axis=0)

    wt, _ = lax.optimization_barrier((conv_weight.T, half))
    wx = lax.all_gather(wt, "x", axis=0)

    near = shift_cores(wx, 1)
    part = jnp.where(first, wx[: NX // 2], wx[NX // 2 :])
    two = shift_cores(part, 2)
    bias = jnp.concatenate([bias_in, bias_out])
    p_in, p_out, bias, _ = lax.optimization_barrier((proj_in.T, proj_out, bias, part))
    p_in_o, p_out_o, bias_o = [shift(v, "c", 2, 1) for v in (p_in, p_out, bias)]
    near_o = shift(near, "c", 2, 1)
    two, bias_o = lax.optimization_barrier((two, bias_o))
    two_o = shift(two, "c", 2, 1)
    hid, later = embed_hidden(
        px,
        (wx, near, near_o, two, two_o),
        p_in,
        p_in_o,
        norm_gain,
        norm_bias,
        bias,
        bias_o,
    )
    hs = ring(lax.all_gather(hid, "zh", axis=0))
    o_own, o_oth = project_out(hs, p_out, p_out_o, later)
    o_got = lax.all_gather(o_oth, "c", axis=0)
    result = jnp.stack([jnp.where(first, o_own, o_got[0]), jnp.where(first, o_got[1], o_own)])
    return result.reshape(2, 16, 16, 256)


def solution(mesh):
    fine = Mesh(mesh.devices.reshape(NX, NZ, 2, NY, 2), ("x", "zl", "zh", "y", "c"))
    tm, tp = ("x", "zl"), ("zh", "y", "c")
    return jax.shard_map(
        per_device,
        mesh=fine,
        in_specs=(
            P(tm, tp, None, None),
            P(None, tm),
            P(),
            P(),
            P(None, tp),
            P(tp),
            P(None, tp),
            P(tp),
        ),
        out_specs=P(tm, None, None, tp),
        check_vma=False,
    )
```
